768 devices in a mesh: blk: 24 (over y, z_hi), row: 32 (over x, z_lo, core).
Axes of the slice: x: 4, y: 8, z: 12 (z_hi: 3, z_lo: 4; z = z_hi * 4 + z_lo), core: 2. Of those that a mesh axis runs over, the one named last changes fastest.
Arguments:
- features: float32 [64, 98304], P(None, ('blk', 'row')), may hold values from -6 to 6
- reorder: int32 [768, 128], P(('blk', 'row')), may hold values from 0 to 127, each once within a row
- tile_rows: int32 [24, 32, 64], P('blk', 'row'), may hold values from 0 to 31
- tile_cols: int32 [24, 32, 64], P('blk', 'row'), may hold values from 0 to 23
- tile_vals: float32 [24, 32, 64, 128, 128], P('blk', 'row')
- tile_count: int32 [24, 32], P('blk', 'row'), may hold values from 1 to 64, as said below
Outputs:
- hop_one: float32 [64, 98304], P(None, ('blk', 'row'))
- hop_two: float32 [64, 98304], P(None, ('blk', 'row'))
The draws below stay inside these ranges and needn't reach their ends.
Inputs may be any that keep to these rules, and one draw needn't show every extreme that they name: `tile_count`: some device has all 64 slots live.
All inputs are finite; a program needn't handle non-finite values.
Results may differ from the reference program's by a relative error of at most 0.0003.
Values sent between devices are 32-bit elements; how exact they have to be, the bound alone decides.
A program may use at most 32 MiB of HBM per device.

```python
import jax
import jax.numpy as jnp
from jax import lax

FEAT = 64
TILE = 128
ROWS_DEV = 128
TILES_DEV = 64
SLICES = 768
NODES = 98304
ROW_TILES = 32
COL_TILES = 24
N_BLK = 24
N_ROW = 32


def draw_tile_vals(key, part):
    key = jax.random.fold_in(key, 5)
    key_diag, key_off, key_scale = jax.random.split(key, 3)
    shape = (N_BLK, N_ROW, TILES_DEV, TILE, TILE)
    diag = jax.random.uniform(key_diag, shape[:-1], jnp.float32, 0.5, 1.5)
    off = jax.random.normal(key_off, shape, jnp.float32) * (0.4 / TILE ** 0.5)
    scale = jnp.exp(jax.random.uniform(key_scale, shape[:-1], jnp.float32, -1.15, 1.15))
    eye = jnp.eye(TILE, dtype=jnp.float32)
    tiles = (off + diag[..., None] * eye) * scale[..., None]
    return 0.3 * tiles


def draw_tile_count(key, part):
    key = jax.random.fold_in(key, 7)
    key_count, key_full = jax.random.split(key)
    counts = jax.random.randint(key_count, (N_BLK * N_ROW,), TILES_DEV // 4, TILES_DEV + 1)
    chosen = jax.random.randint(key_full, (), 0, N_BLK * N_ROW)
    counts = counts.at[chosen].set(TILES_DEV)
    return counts.reshape(N_BLK, N_ROW).astype(jnp.int32)


def place_ends(drawn, rng, smallest, high):
    longest = drawn.shape.index(max(drawn.shape))
    spots = []
    for shift in (0, 1):
        where = [jax.random.randint(jax.random.fold_in(rng, axis), (), 0, length) for axis, length in enumerate(drawn.shape)]
        where[longest] = (where[longest] + shift) % drawn.shape[longest]
        spots.append(tuple(where))
    return drawn.at[spots[0]].set(smallest).at[spots[1]].set(high)


def steps_of(key, dims, pieces, least, high):
    def one(axis_at, shards_of):
        draws = jax.random.uniform(jax.random.fold_in(jax.random.fold_in(key, 6), axis_at), (shards_of,), jnp.float32, least / len(pieces), high / len(pieces))
        return jnp.repeat(jnp.exp(draws), dims[axis_at] // shards_of).reshape((-1,) + (1,) * (len(dims) - axis_at - 1))

    loudness = one(*pieces[0])
    for cut in pieces[1:]:
        loudness = loudness * one(*cut)
    return loudness


def gaussian(rng, dims, width, reach, cuts=(), kind=jnp.bfloat16):
    array = width * jax.random.normal(rng, dims, jnp.float32)
    if cuts:
        array = array * steps_of(rng, dims, cuts, -0.22, 0.18)
    return jnp.clip(array, -reach, reach).astype(kind)


def setup_inputs(seed: int = 0) -> dict:
    keys = jax.random.split(jax.random.key(seed), 7)
    features = gaussian(keys[0], (FEAT, NODES), 1.0, 6.0, ((1, 768),), jnp.float32)
    reorder = jax.vmap(lambda own: jax.random.permutation(own, ROWS_DEV))(jax.random.split(keys[1], SLICES)).reshape((SLICES, ROWS_DEV)).astype(jnp.int32)
    tile_rows = place_ends(jax.random.randint(keys[2], (N_BLK, N_ROW, TILES_DEV), 0, ROW_TILES), jax.random.fold_in(keys[2], 1), 0, ROW_TILES - 1).astype(jnp.int32)
    tile_cols = place_ends(jax.random.randint(keys[3], (N_BLK, N_ROW, TILES_DEV), 0, COL_TILES), jax.random.fold_in(keys[3], 1), 0, COL_TILES - 1).astype(jnp.int32)
    tile_vals = draw_tile_vals(jax.random.fold_in(keys[6], 71), 0)
    tile_count = draw_tile_count(jax.random.fold_in(keys[6], 71), 0)
    return {"features": features, "reorder": reorder, "tile_rows": tile_rows, "tile_cols": tile_cols, "tile_vals": tile_vals, "tile_count": tile_count}


def device_term(rows, cols, vals, count, panel):
    live = (jnp.arange(TILES_DEV) < count).astype(jnp.float32)
    picked = panel[:, cols, :]
    contrib = jnp.einsum("ftj,tij->fti", picked, vals, precision=lax.Precision.HIGHEST)
    contrib = contrib * live[None, :, None]
    onehot = (rows[:, None] == jnp.arange(ROW_TILES)[None, :]).astype(jnp.float32)
    placed = jnp.einsum("fti,tr->fri", contrib, onehot, precision=lax.Precision.HIGHEST)
    return placed.reshape(FEAT, ROW_TILES * TILE)


def propagate(field, tile_rows, tile_cols, tile_vals, tile_count):
    grid = field.reshape(FEAT, N_BLK, N_ROW, ROWS_DEV)
    panels = jnp.moveaxis(grid, 2, 0).reshape(N_ROW, FEAT, COL_TILES, TILE)
    inner = jax.vmap(device_term, in_axes=(0, 0, 0, 0, None))
    outer = jax.vmap(inner, in_axes=(1, 1, 1, 1, 0))
    terms = outer(tile_rows, tile_cols, tile_vals, tile_count, panels)
    summed = jnp.sum(terms, axis=0)
    return jnp.moveaxis(summed, 0, 1).reshape(FEAT, NODES)


def reference(features, reorder, tile_rows, tile_cols, tile_vals, tile_count):
    grid = features.reshape(FEAT, SLICES, ROWS_DEV)
    slice_ids = jnp.arange(SLICES).astype(jnp.int32)[:, None]
    reordered = grid[:, slice_ids, reorder].reshape(FEAT, NODES)
    first = propagate(reordered, tile_rows, tile_cols, tile_vals, tile_count)
    second = propagate(first, tile_rows, tile_cols, tile_vals, tile_count)

    def restore(field):
        empty = jnp.zeros((FEAT, SLICES, ROWS_DEV), jnp.float32)
        return empty.at[:, slice_ids, reorder].set(field.reshape(FEAT, SLICES, ROWS_DEV)).reshape(FEAT, NODES)

    return restore(first), restore(second)
```

```python
import jax
import jax.numpy as jnp
from jax import lax
from jax.experimental import pallas as pl
from jax.experimental.pallas import tpu as pltpu
from jax.sharding import PartitionSpec as P

MESH = pl.DeviceIdType.MESH
F32 = jnp.float32
BF16 = jnp.bfloat16
NY, NZH, NX, NZL = 8, 3, 4, 4
SLOTS = 64
FEAT = 64
TILE = 128
FAR = (4,)
NEAR = tuple(d for d in range(1, NY) if d not in FAR)


def device(y, zh, x, zl, core):
    return (y * NZH + zh, (x * NZL + zl) * 2 + core)


def kernel(feat_hbm, reorder_hbm, rows_hbm, cols_hbm, count_hbm, vals_hbm,
           hop1_ref, hop2_ref,
           feat, reorder, rows, cols, count, vals, table, plan, weights,
           panel, split, seg, send_a, got_a, own_a, send_b, got_b, keep_b, send_c, got_c,
           in_sem, val_sem, plan_sem,
           s_z, r_z, s_y, r_y, r_far, s_ry, r_ry, s_rz, r_rz,
           s_a, r_a, s_b, r_b, s_c, r_c):
    blk = lax.axis_index("blk")
    row = lax.axis_index("row")
    y, zh = blk // NZH, lax.rem(blk, NZH)
    x, zl, core = row // (2 * NZL), lax.rem(row // 2, NZL), lax.rem(row, 2)

    def y_peer(d):
        return device(lax.rem(y + d, NY), zh, x, zl, core)

    def zh_peer(d):
        return device(y, lax.rem(zh + d, NZH), x, zl, core)

    def x_peer(d):
        return device(y, zh, lax.rem(x + d, NX), zl, core)

    def zl_peer(d):
        return device(y, zh, x, lax.rem(zl + d, NZL), core)

    sibling = device(y, zh, x, zl, 1 - core)
    peers = ([y_peer(d) for d in range(1, NY)] + [zh_peer(d) for d in range(1, NZH)] + [x_peer(d) for d in range(1, NX)]
             + [zl_peer(d) for d in range(1, NZL)] + [sibling])
    barrier = pltpu.get_barrier_semaphore()
    for peer in peers:
        pl.semaphore_signal(barrier, inc=1, device_id=peer, device_id_type=MESH)

    loads = [
        pltpu.make_async_copy(feat_hbm, feat, in_sem.at[0]),
        pltpu.make_async_copy(reorder_hbm, reorder, in_sem.at[1]),
        pltpu.make_async_copy(rows_hbm, rows, in_sem.at[2]),
        pltpu.make_async_copy(cols_hbm, cols, in_sem.at[3]),
        pltpu.make_async_copy(count_hbm, count, in_sem.at[4]),
    ]
    for load in loads:
        load.start()
    halves = [pltpu.make_async_copy(vals_hbm.at[0, 0, pl.ds(h * 32, 32)], vals.at[pl.ds(h * 32, 32)], val_sem.at[h])
              for h in range(2)]
    for load in halves:
        load.start()
    for load in loads:
        load.wait()

    onehot = (lax.broadcasted_iota(jnp.int32, (TILE, TILE), 0) == reorder[...]).astype(F32)
    panel[0, blk] = lax.dot_general(feat[...], onehot, (((1,), (0,)), ((), ())), precision=lax.Precision.HIGHEST,
                                    preferred_element_type=F32)
    pl.semaphore_wait(barrier, len(peers))

    def remote(src, dst, send, recv, peer):
        return pltpu.make_async_remote_copy(src_ref=src, dst_ref=dst, send_sem=send, recv_sem=recv, device_id=peer,
                                            device_id_type=MESH)

    def await_bytes(ref, sem):
        pltpu.make_async_copy(ref, ref, sem).wait()

    def gather_own(h):
        mine = panel.at[h, blk]
        for d in range(1, NZH):
            remote(mine, mine, s_z.at[h], r_z.at[h], zh_peer(d)).start()
        for d in (4, 3, 5, 2, 6, 1, 7):
            recv = r_far.at[h, FAR.index(d)] if d in FAR else r_y.at[h]
            remote(mine, mine, s_y.at[h], recv, y_peer(d)).start()

    def gather_relay_y(h):
        await_bytes(panel.at[h, pl.ds(0, NZH - 1)], r_z.at[h])
        for d in sorted(NEAR, key=lambda d: -min(d, NY - d)):
            for e in range(1, NZH):
                block = panel.at[h, y * NZH + lax.rem(zh + e, NZH)]
                remote(block, block, s_ry.at[h], r_ry.at[h], y_peer(d)).start()

    def gather_relay_z(h):
        for n, d in enumerate(FAR):
            await_bytes(panel.at[h, 0], r_far.at[h, n])
            block = panel.at[h, lax.rem(y + NY - d, NY) * NZH + zh]
            for e in range(1, NZH):
                remote(block, block, s_rz.at[h], r_rz.at[h], zh_peer(e)).start()

    def gather_end(h):
        await_bytes(panel.at[h, pl.ds(0, len(NEAR))], r_y.at[h])
        await_bytes(panel.at[h, pl.ds(0, 2 * len(FAR))], r_rz.at[h])
        await_bytes(panel.at[h, pl.ds(0, 2 * len(NEAR))], r_ry.at[h])

    def split_panel(h):
        def one(c, carry):
            block = panel[h, c]
            high = block.astype(BF16)
            split[c, :, 0:TILE] = high
            split[c, :, TILE:2 * TILE] = (block - high.astype(F32)).astype(BF16)
            return carry
        lax.fori_loop(0, NY * NZH, one, 0, unroll=4)

    def prepare(first):
        def one(t, carry):
            tile = vals[t].T
            high = tile.astype(BF16)
            weights[t, :, 0:TILE] = high
            weights[t, :, TILE:2 * TILE] = (tile - high.astype(F32)).astype(BF16)
            return carry
        lax.fori_loop(first, first + 32, one, 0, unroll=4)

    def plan_slots():
        lane = lax.broadcasted_iota(jnp.int32, (1, TILE), 1)
        padded = jnp.concatenate([rows[0], jnp.zeros((1, TILE - SLOTS), jnp.int32)], axis=1)
        group = jnp.where(lane < count[0, 0], padded, 32)
        key = group * SLOTS + lane + jnp.where(lane < SLOTS, 0, 4096)
        across = jnp.broadcast_to(key, (TILE, TILE))
        down = across.T
        rank = jnp.sum(jnp.where(across < down, 1, 0), axis=1, keepdims=True)
        lanes = lax.broadcasted_iota(jnp.int32, (TILE, TILE), 1)
        order = jnp.sum(jnp.where(rank == lanes, down, 0), axis=0, keepdims=True)
        upto = jnp.sum(jnp.where(down < (lanes + 1) * SLOTS, 1, 0), axis=0, keepdims=True)
        before = jnp.sum(jnp.where(down < lanes * SLOTS, 1, 0), axis=0, keepdims=True)
        table[0:1, :] = order
        table[1:2, :] = jnp.maximum(upto - 1, 0)
        table[2:3, :] = upto - before
        copy = pltpu.make_async_copy(table, plan, plan_sem)
        copy.start()
        return copy

    def multiply():
        def one(k, carry):
            total, last = carry
            key = plan[0, k]
            slot = key & (SLOTS - 1)
            group = key >> 6
            column = jnp.clip(cols[0, 0, slot], 0, NY * NZH - 1)
            left = split[column]
            tile = weights[slot]
            both = lax.dot_general(left, jnp.concatenate([tile, tile], axis=0), (((1,), (0,)), ((), ())),
                                   preferred_element_type=F32)
            term = both[:, 0:TILE] + both[:, TILE:2 * TILE]
            total = jnp.where(group == last, total, 0.0) + term
            seg[k] = total
            return total, group
        lax.fori_loop(0, SLOTS, one, (jnp.zeros((FEAT, TILE), F32), jnp.int32(-1)), unroll=8)

    def row_total(r):
        return jnp.where(plan[2, r] > 0, seg[plan[1, r] & (SLOTS - 1)], 0.0)

    def scatter_sum(h):
        for n in range(NZL):
            zt = lax.rem(zl + n + 1, NZL)
            for xt in range(NX):
                r = (xt * NZL + zt) * 2
                send_a[h, n, xt] = row_total(r + 1 - core)
                own_a[n, xt] = row_total(r + core)
            remote(send_a.at[h, n], got_a.at[h, n], s_a.at[h], r_a.at[h, n], sibling).start()
        for n in range(NZL):
            await_bytes(got_a.at[h, n], r_a.at[h, n])
            for d in (2, 1, 3):
                xt = lax.rem(x + d, NX)
                send_b[h, n, d - 1] = own_a[n, xt] + got_a[h, n, xt]
                remote(send_b.at[h, n, d - 1], got_b.at[h, n, d - 1], s_b.at[h], r_b.at[h, n], x_peer(d)).start()
            keep_b[n] = own_a[n, x] + got_a[h, n, x]
        for n in range(NZL):
            await_bytes(got_b.at[h, n], r_b.at[h, n])
            part = (keep_b[n] + got_b[h, n, 0]) + (got_b[h, n, 1] + got_b[h, n, 2])
            if n < NZL - 1:
                send_c[h, n] = part
                remote(send_c.at[h, n], got_c.at[h, n], s_c.at[h], r_c.at[h], zl_peer(n + 1)).start()
        await_bytes(got_c.at[h], r_c.at[h])
        return part + (got_c[h, 0] + got_c[h, 1] + got_c[h, 2])

    def sends_end(h):
        await_bytes(panel.at[h, pl.ds(0, NZH - 1)], s_z.at[h])
        await_bytes(panel.at[h, pl.ds(0, NY - 1)], s_y.at[h])
        await_bytes(panel.at[h, pl.ds(0, 2 * len(NEAR))], s_ry.at[h])
        await_bytes(panel.at[h, pl.ds(0, 2 * len(FAR))], s_rz.at[h])
        await_bytes(send_a.at[h], s_a.at[h])
        await_bytes(send_b.at[h], s_b.at[h])
        await_bytes(send_c.at[h], s_c.at[h])

    def restored(field):
        return lax.dot_general(field, onehot, (((1,), (1,)), ((), ())), precision=lax.Precision.HIGHEST,
                               preferred_element_type=F32)

    gather_own(0)
    copy = plan_slots()
    halves[0].wait()
    prepare(0)
    gather_relay_y(0)
    gather_relay_z(0)
    halves[1].wait()
    prepare(32)
    copy.wait()
    gather_end(0)
    split_panel(0)
    multiply()
    first = scatter_sum(0)
    panel[1, blk] = first
    gather_own(1)
    hop1_ref[...] = restored(first)
    gather_relay_y(1)
    gather_relay_z(1)
    gather_end(1)
    split_panel(1)
    multiply()
    second = scatter_sum(1)
    hop2_ref[...] = restored(second)
    sends_end(0)
    sends_end(1)


def shards(features, reorder, tile_rows, tile_cols, tile_vals, tile_count):
    dma = pltpu.SemaphoreType.DMA
    block = (FEAT, TILE)
    return pl.pallas_call(
        kernel,
        name="two_hops",
        out_shape=(jax.ShapeDtypeStruct(block, F32), jax.ShapeDtypeStruct(block, F32)),
        in_specs=[pl.BlockSpec(memory_space=pltpu.HBM)] * 6,
        out_specs=(pl.BlockSpec(memory_space=pltpu.VMEM), pl.BlockSpec(memory_space=pltpu.VMEM)),
        scratch_shapes=[
            pltpu.VMEM(block, F32),
            pltpu.VMEM((1, TILE), jnp.int32),
            pltpu.VMEM((1, 1, SLOTS), jnp.int32),
            pltpu.SMEM((1, 1, SLOTS), jnp.int32),
            pltpu.SMEM((1, 1), jnp.int32),
            pltpu.VMEM((SLOTS, TILE, TILE), F32),
            pltpu.VMEM((8, TILE), jnp.int32),
            pltpu.SMEM((8, TILE), jnp.int32),
            pltpu.VMEM((SLOTS, TILE, 2 * TILE), BF16),
            pltpu.VMEM((2, NY * NZH) + block, F32),
            pltpu.VMEM((NY * NZH, FEAT, 2 * TILE), BF16),
            pltpu.VMEM((SLOTS,) + block, F32),
            pltpu.VMEM((2, NZL, NX) + block, F32),
            pltpu.VMEM((2, NZL, NX) + block, F32),
            pltpu.VMEM((NZL, NX) + block, F32),
            pltpu.VMEM((2, NZL, NX - 1) + block, F32),
            pltpu.VMEM((2, NZL, NX - 1) + block, F32),
            pltpu.VMEM((NZL,) + block, F32),
            pltpu.VMEM((2, NZL - 1) + block, F32),
            pltpu.VMEM((2, NZL - 1) + block, F32),
            dma((5,)), dma((2,)), dma,
            dma((2,)), dma((2,)), dma((2,)), dma((2,)), dma((2, len(FAR))), dma((2,)), dma((2,)), dma((2,)), dma((2,)),
            dma((2,)), dma((2, NZL)), dma((2,)), dma((2, NZL)), dma((2,)), dma((2,)),
        ],
        compiler_params=pltpu.CompilerParams(collective_id=0, has_side_effects=True, vmem_limit_bytes=56 << 20),
        cost_estimate=pl.CostEstimate(flops=2 * 2 * 64 * 64 * 128 * 128 * 4, bytes_accessed=4 << 20, transcendentals=0),
    )(features, reorder, tile_rows, tile_cols, tile_count, tile_vals)


def solution(mesh):
    return jax.shard_map(
        shards,
        mesh=mesh,
        in_specs=(
            P(None, ("blk", "row")),
            P(("blk", "row"), None),
            P("blk", "row", None),
            P("blk", "row", None),
            P("blk", "row", None, None, None),
            P("blk", "row"),
        ),
        out_specs=(P(None, ("blk", "row")), P(None, ("blk", "row"))),
        check_vma=False,
    )
```

```python
import jax
import jax.numpy as jnp
from jax import lax
from jax.experimental import pallas as pl
from jax.experimental.pallas import tpu as pltpu
from jax.sharding import PartitionSpec as P

MESH = pl.DeviceIdType.MESH
F32 = jnp.float32
BF16 = jnp.bfloat16
NY, NZH, NX, NZL = 8, 3, 4, 4
SLOTS = 64
FEAT = 64
TILE = 128
FAR = (4, 3, 5)
NEAR = (2, 6, 1, 7)


def device(y, zh, x, zl, core):
    return (y * NZH + zh, (x * NZL + zl) * 2 + core)


def kernel(feat_hbm, reorder_hbm, rows_hbm, cols_hbm, count_hbm, vals_hbm,
           out_ref,
           feat, reorder, rows, cols, count, vals, table, plan, weights,
           panel, split, seg, send_a, got_a, send_b, got_b, keep_b, send_c, got_c,
           in_sem, val_sem, plan_sem,
           s_g, r_z, r_far, r_near, r_relay, s_a, r_a, s_b, r_b, s_c, r_c):
    blk = lax.axis_index("blk")
    row = lax.axis_index("row")
    y, zh = blk // NZH, lax.rem(blk, NZH)
    x, zl, core = row >> 3, (row >> 1) & (NZL - 1), row & 1
    order = (jnp.where(zl < 2, 3, 0), jnp.where(zl < 2, 2, 1),
             jnp.where(zl == 0, 1, jnp.where(zl == 1, 0, jnp.where(zl == 2, 3, 2))), zl)

    def y_peer(d):
        return device((y + d) & (NY - 1), zh, x, zl, core)

    def zh_peer(d):
        return device(y, jnp.where(zh + d >= NZH, zh + d - NZH, zh + d), x, zl, core)

    def x_peer(d):
        return device(y, zh, (x + d) & (NX - 1), zl, core)

    def zl_peer(t):
        return device(y, zh, x, t, core)

    sibling = device(y, zh, x, zl, 1 - core)
    loads = [
        pltpu.make_async_copy(feat_hbm, feat, in_sem.at[0]),
        pltpu.make_async_copy(reorder_hbm, reorder, in_sem.at[1]),
        pltpu.make_async_copy(rows_hbm, rows, in_sem.at[2]),
        pltpu.make_async_copy(cols_hbm, cols, in_sem.at[3]),
        pltpu.make_async_copy(count_hbm, count, in_sem.at[4]),
    ]
    loads[0].start()
    loads[1].start()
    peers = ([zh_peer(d) for d in range(1, NZH)] + [y_peer(d) for d in (4, 3, 5, 2, 6, 1, 7)] + [zl_peer(t) for t in order[:-1]]
             + [x_peer(d) for d in (2, 1, 3)] + [sibling])
    barrier = pltpu.get_barrier_semaphore()
    for peer in peers:
        pl.semaphore_signal(barrier, inc=1, device_id=peer, device_id_type=MESH)
    for load in loads[2:]:
        load.start()
    halves = [pltpu.make_async_copy(vals_hbm.at[0, 0, pl.ds(h * 32, 32)], vals.at[pl.ds(h * 32, 32)], val_sem.at[h])
              for h in range(2)]
    for load in halves:
        load.start()
    loads[0].wait()
    loads[1].wait()

    onehot = (lax.broadcasted_iota(jnp.int32, (TILE, TILE), 0) == reorder[...]).astype(F32)
    panel[0, 0, y] = lax.dot_general(feat[...], onehot, (((1,), (0,)), ((), ())), precision=lax.Precision.HIGHEST,
                                     preferred_element_type=F32)
    pl.semaphore_wait(barrier, len(peers))

    def remote(src, dst, send, recv, peer):
        return pltpu.make_async_remote_copy(src_ref=src, dst_ref=dst, send_sem=send, recv_sem=recv, device_id=peer,
                                            device_id_type=MESH)

    def await_bytes(ref, sem):
        pltpu.make_async_copy(ref, ref, sem).wait()

    def gather_own(h):
        mine = panel.at[h, 0, y]
        for e in range(1, NZH):
            remote(mine, panel.at[h, NZH - e, y], s_g.at[h], r_z.at[h], zh_peer(e)).start()
        for d in FAR + NEAR:
            recv = r_far.at[h, FAR.index(d)] if d in FAR else r_near.at[h]
            remote(mine, mine, s_g.at[h], recv, y_peer(d)).start()

    def gather_relay(h):
        await_bytes(panel.at[h, 0, pl.ds(0, NZH - 1)], r_z.at[h])
        for d, e in ((3, 2), (5, 1)):
            ref = panel.at[h, e, y]
            remote(ref, ref, s_g.at[h], r_relay.at[h], y_peer(d)).start()
        pair = panel.at[h, pl.ds(1, NZH - 1), y]
        for d in NEAR:
            remote(pair, pair, s_g.at[h], r_relay.at[h], y_peer(d)).start()
        for n, d, es in ((0, 4, (1, 2)), (1, 3, (2,)), (2, 5, (1,))):
            await_bytes(panel.at[h, 0, 0], r_far.at[h, n])
            k = (y + NY - d) & (NY - 1)
            for e in es:
                remote(panel.at[h, 0, k], panel.at[h, NZH - e, k], s_g.at[h], r_relay.at[h], zh_peer(e)).start()

    def split_panel(h, first, count):
        def one(k, carry):
            block = panel[h, k >> 3, k & (NY - 1)]
            high = block.astype(BF16)
            split[k, :, 0:TILE] = high
            split[k, :, TILE:2 * TILE] = (block - high.astype(F32)).astype(BF16)
            return carry
        lax.fori_loop(first, first + count, one, 0, unroll=8)

    def gather_end(h):
        await_bytes(panel.at[h, 0, pl.ds(0, len(NEAR))], r_near.at[h])
        split_panel(h, 0, NY)
        await_bytes(panel.at[h, pl.ds(1, NZH - 1), pl.ds(0, NY - 1)], r_relay.at[h])
        split_panel(h, NY, (NZH - 1) * NY)

    def prepare(first):
        def one(t, carry):
            tile = vals[t].T
            high = tile.astype(BF16)
            weights[t, :, 0:TILE] = high
            weights[t, :, TILE:2 * TILE] = (tile - high.astype(F32)).astype(BF16)
            return carry
        lax.fori_loop(first, first + 32, one, 0, unroll=4)

    def plan_slots():
        for load in loads[2:]:
            load.wait()
        lane = lax.broadcasted_iota(jnp.int32, (1, TILE), 1)
        pad = jnp.zeros((1, TILE - SLOTS), jnp.int32)
        group = jnp.where(lane < count[0, 0], jnp.concatenate([rows[0], pad], axis=1), 32)
        column = jnp.concatenate([cols[0], pad], axis=1)
        column_y = (column * 43) >> 7
        ahead = column - NZH * column_y - zh
        place = jnp.where(ahead < 0, ahead + NZH, ahead) * NY + column_y
        key = (group * TILE + lane) * 32 + place
        across = jnp.broadcast_to(key, (TILE, TILE))
        down = across.T
        rank = jnp.sum(jnp.where(across < down, 1, 0), axis=1, keepdims=True)
        lanes = lax.broadcasted_iota(jnp.int32, (TILE, TILE), 1)
        ordered = jnp.sum(jnp.where(rank == lanes, down, 0), axis=0, keepdims=True)
        upto = jnp.sum(jnp.where(down < (lanes + 1) * (TILE * 32), 1, 0), axis=0, keepdims=True)
        before = jnp.sum(jnp.where(down < lanes * (TILE * 32), 1, 0), axis=0, keepdims=True)
        table[0:1, :] = ordered
        table[1:2, :] = jnp.where(upto > before, upto - 1, SLOTS)

    def multiply():
        def one(k, carry):
            total, last = carry
            key = plan[0, k]
            group = key >> 12
            tile = weights[(key >> 5) & (SLOTS - 1)]
            left = split[jnp.minimum(key & 31, NY * NZH - 1)]
            high, low = tile[:, 0:TILE], tile[:, TILE:2 * TILE]
            term = lax.dot_general(left, jnp.concatenate([high, high], axis=0), (((1,), (0,)), ((), ())),
                                   preferred_element_type=F32)
            term = term + lax.dot_general(left[:, 0:TILE], low, (((1,), (0,)), ((), ())), preferred_element_type=F32)
            total = jnp.where(group == last, total, 0.0) + term
            seg[k] = total
            return total, group
        lax.fori_loop(0, SLOTS, one, (jnp.zeros((FEAT, TILE), F32), jnp.int32(-1)), unroll=32)

    def row_total(r):
        return seg[jnp.minimum(plan[1, r] & (TILE - 1), SLOTS)]

    def scatter_sum(h):
        for n, zt in enumerate(order):
            for xt in range(NX):
                send_a[h, n, xt] = row_total((xt * NZL + zt) * 2 + 1 - core)
            remote(send_a.at[h, n], got_a.at[h, n], s_a.at[h], r_a.at[h, n], sibling).start()
        for n, zt in enumerate(order):
            await_bytes(got_a.at[h, n], r_a.at[h, n])
            for d in (2, 1, 3):
                xt = (x + d) & (NX - 1)
                send_b[h, n, d - 1] = row_total((xt * NZL + zt) * 2 + core) + got_a[h, n, xt]
                remote(send_b.at[h, n, d - 1], got_b.at[h, n, d - 1], s_b.at[h], r_b.at[h, n], x_peer(d)).start()
            keep_b[n] = row_total((x * NZL + zt) * 2 + core) + got_a[h, n, x]
        for n, zt in enumerate(order):
            await_bytes(got_b.at[h, n], r_b.at[h, n])
            part = (keep_b[n] + got_b[h, n, 0]) + (got_b[h, n, 1] + got_b[h, n, 2])
            if n < NZL - 1:
                send_c[h, n] = part
                there = ((zl - zt + NZL) & (NZL - 1)) - 1
                remote(send_c.at[h, n], got_c.at[h, there], s_c.at[h], r_c.at[h], zl_peer(zt)).start()
        await_bytes(got_c.at[h], r_c.at[h])
        return part + (got_c[h, 0] + got_c[h, 1] + got_c[h, 2])

    def sends_end(h):
        await_bytes(panel.at[h, :, pl.ds(0, NY - 1)], s_g.at[h])
        await_bytes(panel.at[h, pl.ds(0, NZH - 1), 0], s_g.at[h])
        await_bytes(send_a.at[h], s_a.at[h])
        await_bytes(send_b.at[h], s_b.at[h])
        await_bytes(send_c.at[h], s_c.at[h])

    seg[SLOTS] = jnp.zeros((FEAT, TILE), F32)
    plan_copy = pltpu.make_async_copy(table, plan, plan_sem)

    def hop(h, carry):
        gather_own(h)

        @pl.when(h == 0)
        def _():
            plan_slots()
            plan_copy.start()
            halves[0].wait()
            prepare(0)

        gather_relay(h)

        @pl.when(h == 0)
        def _():
            halves[1].wait()
            prepare(32)
            plan_copy.wait()

        gather_end(h)
        multiply()
        field = scatter_sum(h)
        out_ref[h] = field

        @pl.when(h == 0)
        def _():
            panel[1, 0, y] = field

        return carry

    lax.fori_loop(0, 2, hop, 0)
    sends_end(0)
    sends_end(1)


def restore(fields_hbm, reorder_hbm, hop1_ref, hop2_ref, fields, reorder, sems):
    loads = [pltpu.make_async_copy(reorder_hbm, reorder, sems.at[0]), pltpu.make_async_copy(fields_hbm, fields, sems.at[1])]
    for load in loads:
        load.start()
    loads[0].wait()
    onehot = (lax.broadcasted_iota(jnp.int32, (TILE, TILE), 0) == reorder[...]).astype(F32)
    loads[1].wait()
    for n, hop in enumerate((hop1_ref, hop2_ref)):
        hop[...] = lax.dot_general(fields[n], onehot, (((1,), (1,)), ((), ())), precision=lax.Precision.HIGHEST,
                                   preferred_element_type=F32)


def shards(features, reorder, tile_rows, tile_cols, tile_vals, tile_count):
    dma = pltpu.SemaphoreType.DMA
    block = (FEAT, TILE)
    shape = jax.ShapeDtypeStruct(block, F32)
    fields = pl.pallas_call(
        kernel,
        name="two_hops",
        out_shape=jax.ShapeDtypeStruct((2,) + block, F32),
        in_specs=[pl.BlockSpec(memory_space=pltpu.HBM)] * 6,
        out_specs=pl.BlockSpec(memory_space=pltpu.VMEM),
        scratch_shapes=[
            pltpu.VMEM(block, F32),
            pltpu.VMEM((1, TILE), jnp.int32),
            pltpu.VMEM((1, 1, SLOTS), jnp.int32),
            pltpu.VMEM((1, 1, SLOTS), jnp.int32),
            pltpu.SMEM((1, 1), jnp.int32),
            pltpu.VMEM((SLOTS, TILE, TILE), F32),
            pltpu.VMEM((8, TILE), jnp.int32),
            pltpu.SMEM((8, TILE), jnp.int32),
            pltpu.VMEM((SLOTS, TILE, 2 * TILE), BF16),
            pltpu.VMEM((2, NZH, NY) + block, F32),
            pltpu.VMEM((NY * NZH, FEAT, 2 * TILE), BF16),
            pltpu.VMEM((SLOTS + 1,) + block, F32),
            pltpu.VMEM((2, NZL, NX) + block, F32),
            pltpu.VMEM((2, NZL, NX) + block, F32),
            pltpu.VMEM((2, NZL, NX - 1) + block, F32),
            pltpu.VMEM((2, NZL, NX - 1) + block, F32),
            pltpu.VMEM((NZL,) + block, F32),
            pltpu.VMEM((2, NZL - 1) + block, F32),
            pltpu.VMEM((2, NZL - 1) + block, F32),
            dma((5,)), dma((2,)), dma,
            dma((2,)), dma((2,)), dma((2, len(FAR))), dma((2,)), dma((2,)),
            dma((2,)), dma((2, NZL)), dma((2,)), dma((2, NZL)), dma((2,)), dma((2,)),
        ],
        compiler_params=pltpu.CompilerParams(collective_id=0, has_side_effects=True, vmem_limit_bytes=56 << 20),
        cost_estimate=pl.CostEstimate(flops=2 * 2 * 64 * 64 * 128 * 128 * 3, bytes_accessed=4 << 20, transcendentals=0),
    )(features, reorder, tile_rows, tile_cols, tile_count, tile_vals)
    return pl.pallas_call(
        restore,
        name="restore",
        out_shape=(shape, shape),
        in_specs=[pl.BlockSpec(memory_space=pltpu.HBM)] * 2,
        out_specs=(pl.BlockSpec(memory_space=pltpu.VMEM), pl.BlockSpec(memory_space=pltpu.VMEM)),
        scratch_shapes=[pltpu.VMEM((2,) + block, F32), pltpu.VMEM((1, TILE), jnp.int32), dma((2,))],
        compiler_params=pltpu.CompilerParams(vmem_limit_bytes=56 << 20),
    )(fields, reorder)


def solution(mesh):
    return jax.shard_map(
        shards,
        mesh=mesh,
        in_specs=(
            P(None, ("blk", "row")),
            P(("blk", "row"), None),
            P("blk", "row", None),
            P("blk", "row", None),
            P("blk", "row", None, None, None),
            P("blk", "row"),
        ),
        out_specs=(P(None, ("blk", "row")), P(None, ("blk", "row"))),
        check_vma=False,
    )
```

```python
import jax
import jax.numpy as jnp
from jax import lax
from jax.experimental import pallas as pl
from jax.experimental.pallas import tpu as pltpu
from jax.sharding import PartitionSpec as P

MESH = pl.DeviceIdType.MESH
F32 = jnp.float32
BF16 = jnp.bfloat16
NY, NZH, NX, NZL = 8, 3, 4, 4
SLOTS = 64
FEAT = 64
TILE = 128
FAR = (4, 3, 5)
NEAR = (2, 6, 1, 7)
PARTS = 2
GROUP = FEAT // PARTS


def device(y, zh, x, zl, core):
    return (y * NZH + zh, (x * NZL + zl) * 2 + core)


def kernel(feat_hbm, reorder_hbm, rows_hbm, cols_hbm, count_hbm, vals_hbm,
           out_ref,
           feat, reorder, rows, cols, count, vals, table, plan, weights,
           panel, split, seg, send_a, got_a, send_b, got_b, send_c, got_c,
           in_sem, val_sem, plan_sem,
           s_g, r_z, r_far, r_near, r_relay, s_a, r_a, s_b, r_b, s_c, r_c):
    blk = lax.axis_index("blk")
    row = lax.axis_index("row")
    y, zh = blk // NZH, lax.rem(blk, NZH)
    x, zl, core = row >> 3, (row >> 1) & (NZL - 1), row & 1
    order = (jnp.where(zl < 2, 3, 0), jnp.where(zl < 2, 2, 1),
             jnp.where(zl == 0, 1, jnp.where(zl == 1, 0, jnp.where(zl == 2, 3, 2))), zl)

    def y_peer(d):
        return device((y + d) & (NY - 1), zh, x, zl, core)

    def zh_peer(d):
        return device(y, jnp.where(zh + d >= NZH, zh + d - NZH, zh + d), x, zl, core)

    def x_peer(d):
        return device(y, zh, (x + d) & (NX - 1), zl, core)

    def zl_peer(t):
        return device(y, zh, x, t, core)

    sibling = device(y, zh, x, zl, 1 - core)
    loads = [
        pltpu.make_async_copy(feat_hbm, feat, in_sem.at[0]),
        pltpu.make_async_copy(reorder_hbm, reorder, in_sem.at[1]),
        pltpu.make_async_copy(rows_hbm, rows, in_sem.at[2]),
        pltpu.make_async_copy(cols_hbm, cols, in_sem.at[3]),
        pltpu.make_async_copy(count_hbm, count, in_sem.at[4]),
    ]
    loads[0].start()
    loads[1].start()
    peers = ([zh_peer(d) for d in range(1, NZH)] + [y_peer(d) for d in (4, 3, 5, 2, 6, 1, 7)] + [zl_peer(t) for t in order[:-1]]
             + [x_peer(d) for d in (2, 1, 3)] + [sibling])
    barrier = pltpu.get_barrier_semaphore()
    for peer in peers:
        pl.semaphore_signal(barrier, inc=1, device_id=peer, device_id_type=MESH)
    for load in loads[2:]:
        load.start()
    halves = [pltpu.make_async_copy(vals_hbm.at[0, 0, pl.ds(h * 32, 32)], vals.at[pl.ds(h * 32, 32)], val_sem.at[h])
              for h in range(2)]
    for load in halves:
        load.start()
    loads[0].wait()
    loads[1].wait()

    onehot = (lax.broadcasted_iota(jnp.int32, (TILE, TILE), 0) == reorder[...]).astype(F32)
    panel[0, 0, y] = lax.dot_general(feat[...], onehot, (((1,), (0,)), ((), ())), precision=lax.Precision.HIGHEST,
                                     preferred_element_type=F32)
    pl.semaphore_wait(barrier, len(peers))

    def remote(src, dst, send, recv, peer):
        return pltpu.make_async_remote_copy(src_ref=src, dst_ref=dst, send_sem=send, recv_sem=recv, device_id=peer,
                                            device_id_type=MESH)

    def await_bytes(ref, sem):
        pltpu.make_async_copy(ref, ref, sem).wait()

    def gather_own(h):
        for f in range(PARTS):
            part = pl.ds(f * GROUP, GROUP)
            mine = panel.at[h, 0, y, part]
            for e in range(1, NZH):
                remote(mine, panel.at[h, NZH - e, y, part], s_g.at[h], r_z.at[h, f], zh_peer(e)).start()
            for n, d in enumerate(FAR):
                remote(mine, mine, s_g.at[h], r_far.at[h, f, n], y_peer(d)).start()
        mine = panel.at[h, 0, y]
        for d in NEAR:
            remote(mine, mine, s_g.at[h], r_near.at[h], y_peer(d)).start()

    def gather_relay(h):
        for f in range(PARTS):
            part = pl.ds(f * GROUP, GROUP)
            await_bytes(panel.at[h, 0, pl.ds(0, NZH - 1), part], r_z.at[h, f])
            for d, e in ((3, 2), (5, 1)):
                ref = panel.at[h, e, y, part]
                remote(ref, ref, s_g.at[h], r_relay.at[h], y_peer(d)).start()
            if f == PARTS - 1:
                pair = panel.at[h, pl.ds(1, NZH - 1), y]
                for d in NEAR:
                    remote(pair, pair, s_g.at[h], r_relay.at[h], y_peer(d)).start()
            for n, d, steps in ((0, 4, (1, 2)), (1, 3, (2,)), (2, 5, (1,))):
                await_bytes(panel.at[h, 0, 0, part], r_far.at[h, f, n])
                k = (y + NY - d) & (NY - 1)
                for e in steps:
                    remote(panel.at[h, 0, k, part], panel.at[h, NZH - e, k, part], s_g.at[h], r_relay.at[h], zh_peer(e)).start()

    def split_panel(h, first, count):
        def one(k, carry):
            block = panel[h, k >> 3, k & (NY - 1)]
            high = block.astype(BF16)
            split[k, :, 0:TILE] = high
            split[k, :, TILE:2 * TILE] = (block - high.astype(F32)).astype(BF16)
            return carry
        lax.fori_loop(first, first + count, one, 0, unroll=8)

    def gather_end(h):
        await_bytes(panel.at[h, 0, pl.ds(0, len(NEAR))], r_near.at[h])
        split_panel(h, 0, NY)
        await_bytes(panel.at[h, pl.ds(1, NZH - 1), pl.ds(0, NY - 1)], r_relay.at[h])
        split_panel(h, NY, (NZH - 1) * NY)

    def prepare(first):
        def one(t, carry):
            tile = vals[t].T
            high = tile.astype(BF16)
            weights[t, :, 0:TILE] = high
            weights[t, :, TILE:2 * TILE] = (tile - high.astype(F32)).astype(BF16)
            return carry
        lax.fori_loop(first, first + 32, one, 0, unroll=4)

    def plan_slots():
        for load in loads[2:]:
            load.wait()
        lane = lax.broadcasted_iota(jnp.int32, (1, TILE), 1)
        pad = jnp.zeros((1, TILE - SLOTS), jnp.int32)
        group = jnp.where(lane < count[0, 0], jnp.concatenate([rows[0], pad], axis=1), 32)
        column = jnp.concatenate([cols[0], pad], axis=1)
        column_y = (column * 43) >> 7
        ahead = column - NZH * column_y - zh
        place = jnp.where(ahead < 0, ahead + NZH, ahead) * NY + column_y
        key = (group * TILE + lane) * 32 + place
        across = jnp.broadcast_to(key, (TILE, TILE))
        down = across.T
        rank = jnp.sum(jnp.where(across < down, 1, 0), axis=1, keepdims=True)
        lanes = lax.broadcasted_iota(jnp.int32, (TILE, TILE), 1)
        ordered = jnp.sum(jnp.where(rank == lanes, down, 0), axis=0, keepdims=True)
        upto = jnp.sum(jnp.where(down < (lanes + 1) * (TILE * 32), 1, 0), axis=0, keepdims=True)
        before = jnp.sum(jnp.where(down < lanes * (TILE * 32), 1, 0), axis=0, keepdims=True)
        table[0:1, :] = ordered
        table[1:2, :] = jnp.where(upto > before, upto - 1, SLOTS)

    def multiply():
        def one(k, carry):
            total, last = carry
            key = plan[0, k]
            group = key >> 12
            tile = weights[(key >> 5) & (SLOTS - 1)]
            left = split[jnp.minimum(key & 31, NY * NZH - 1)]
            high, low = tile[:, 0:TILE], tile[:, TILE:2 * TILE]
            term = lax.dot_general(left, jnp.concatenate([high, high], axis=0), (((1,), (0,)), ((), ())),
                                   preferred_element_type=F32)
            term = term + lax.dot_general(left[:, 0:TILE], low, (((1,), (0,)), ((), ())), preferred_element_type=F32)
            total = jnp.where(group == last, total, 0.0) + term
            seg[k] = total
            return total, group
        lax.fori_loop(0, SLOTS, one, (jnp.zeros((FEAT, TILE), F32), jnp.int32(-1)), unroll=64)

    def row_total(r):
        return seg[jnp.minimum(plan[1, r] & (TILE - 1), SLOTS)]

    def sends_end(h):
        await_bytes(panel.at[h, :, pl.ds(0, NY - 1)], s_g.at[h])
        await_bytes(panel.at[h, pl.ds(0, NZH - 1), 0], s_g.at[h])
        await_bytes(send_a.at[h], s_a.at[h])
        await_bytes(send_b.at[h], s_b.at[h])

    def scatter_sum(h):
        for n, zt in enumerate(order):
            for xt in range(NX):
                send_a[h, n, xt] = row_total((xt * NZL + zt) * 2 + 1 - core)
            if n == 0:
                remote(send_a.at[h, 0], got_a.at[h, 0], s_a.at[h], r_a.at[h, 0], sibling).start()
        rest = pl.ds(1, NZL - 1)
        remote(send_a.at[h, rest], got_a.at[h, rest], s_a.at[h], r_a.at[h, 1], sibling).start()
        for n, zt in enumerate(order):
            if n < 2:
                await_bytes(got_a.at[h, pl.ds(n, 1 if n == 0 else NZL - 1)], r_a.at[h, n])
            for d in (2, 1, 3):
                xt = (x + d) & (NX - 1)
                send_b[h, n, d - 1] = row_total((xt * NZL + zt) * 2 + core) + got_a[h, n, xt]
                remote(send_b.at[h, n, d - 1], got_b.at[h, n, d - 1], s_b.at[h], r_b.at[h, n], x_peer(d)).start()
        for n, zt in enumerate(order):
            kept = row_total((x * NZL + zt) * 2 + core) + got_a[h, n, x]
            await_bytes(got_b.at[h, n], r_b.at[h, n])
            part = (kept + got_b[h, n, 0]) + (got_b[h, n, 1] + got_b[h, n, 2])
            if n < NZL - 1:
                send_c[h, n] = part
                there = ((zl - zt + NZL) & (NZL - 1)) - 1
                remote(send_c.at[h, n], got_c.at[h, there], s_c.at[h], r_c.at[h], zl_peer(zt)).start()
        sends_end(h)
        await_bytes(got_c.at[h], r_c.at[h])
        await_bytes(send_c.at[h], s_c.at[h])
        return part + (got_c[h, 0] + got_c[h, 1] + got_c[h, 2])

    seg[SLOTS] = jnp.zeros((FEAT, TILE), F32)
    plan_copy = pltpu.make_async_copy(table, plan, plan_sem)

    def hop(h, carry):
        gather_own(h)

        @pl.when(h == 0)
        def _():
            plan_slots()
            plan_copy.start()
            halves[0].wait()
            prepare(0)

        gather_relay(h)

        @pl.when(h == 0)
        def _():
            halves[1].wait()
            prepare(32)
            plan_copy.wait()

        gather_end(h)
        multiply()
        field = scatter_sum(h)
        out_ref[h] = field

        @pl.when(h == 0)
        def _():
            panel[1, 0, y] = field

        return carry

    lax.fori_loop(0, 2, hop, 0)


def restore(fields_hbm, reorder_hbm, hop1_ref, hop2_ref, fields, reorder, sems):
    loads = [pltpu.make_async_copy(reorder_hbm, reorder, sems.at[0]), pltpu.make_async_copy(fields_hbm, fields, sems.at[1])]
    for load in loads:
        load.start()
    loads[0].wait()
    onehot = (lax.broadcasted_iota(jnp.int32, (TILE, TILE), 0) == reorder[...]).astype(F32)
    loads[1].wait()
    for n, hop in enumerate((hop1_ref, hop2_ref)):
        hop[...] = lax.dot_general(fields[n], onehot, (((1,), (1,)), ((), ())), precision=lax.Precision.HIGHEST,
                                   preferred_element_type=F32)


def shards(features, reorder, tile_rows, tile_cols, tile_vals, tile_count):
    dma = pltpu.SemaphoreType.DMA
    block = (FEAT, TILE)
    shape = jax.ShapeDtypeStruct(block, F32)
    fields = pl.pallas_call(
        kernel,
        name="two_hops",
        out_shape=jax.ShapeDtypeStruct((2,) + block, F32),
        in_specs=[pl.BlockSpec(memory_space=pltpu.HBM)] * 6,
        out_specs=pl.BlockSpec(memory_space=pltpu.VMEM),
        scratch_shapes=[
            pltpu.VMEM(block, F32),
            pltpu.VMEM((1, TILE), jnp.int32),
            pltpu.VMEM((1, 1, SLOTS), jnp.int32),
            pltpu.VMEM((1, 1, SLOTS), jnp.int32),
            pltpu.SMEM((1, 1), jnp.int32),
            pltpu.VMEM((SLOTS, TILE, TILE), F32),
            pltpu.VMEM((8, TILE), jnp.int32),
            pltpu.SMEM((8, TILE), jnp.int32),
            pltpu.VMEM((SLOTS, TILE, 2 * TILE), BF16),
            pltpu.VMEM((2, NZH, NY) + block, F32),
            pltpu.VMEM((NY * NZH, FEAT, 2 * TILE), BF16),
            pltpu.VMEM((SLOTS + 1,) + block, F32),
            pltpu.VMEM((2, NZL, NX) + block, F32),
            pltpu.VMEM((2, NZL, NX) + block, F32),
            pltpu.VMEM((2, NZL, NX - 1) + block, F32),
            pltpu.VMEM((2, NZL, NX - 1) + block, F32),
            pltpu.VMEM((2, NZL - 1) + block, F32),
            pltpu.VMEM((2, NZL - 1) + block, F32),
            dma((5,)), dma((2,)), dma,
            dma((2,)), dma((2, PARTS)), dma((2, PARTS, len(FAR))), dma((2,)), dma((2,)),
            dma((2,)), dma((2, NZL)), dma((2,)), dma((2, NZL)), dma((2,)), dma((2,)),
        ],
        compiler_params=pltpu.CompilerParams(collective_id=0, has_side_effects=True, vmem_limit_bytes=56 << 20),
        cost_estimate=pl.CostEstimate(flops=2 * 2 * 64 * 64 * 128 * 128 * 3, bytes_accessed=4 << 20, transcendentals=0),
    )(features, reorder, tile_rows, tile_cols, tile_count, tile_vals)
    return pl.pallas_call(
        restore,
        name="restore",
        out_shape=(shape, shape),
        in_specs=[pl.BlockSpec(memory_space=pltpu.HBM)] * 2,
        out_specs=(pl.BlockSpec(memory_space=pltpu.VMEM), pl.BlockSpec(memory_space=pltpu.VMEM)),
        scratch_shapes=[pltpu.VMEM((2,) + block, F32), pltpu.VMEM((1, TILE), jnp.int32), dma((2,))],
        compiler_params=pltpu.CompilerParams(vmem_limit_bytes=56 << 20),
    )(fields, reorder)


def solution(mesh):
    return jax.shard_map(
        shards,
        mesh=mesh,
        in_specs=(
            P(None, ("blk", "row")),
            P(("blk", "row"), None),
            P("blk", "row", None),
            P("blk", "row", None),
            P("blk", "row", None, None, None),
            P("blk", "row"),
        ),
        out_specs=(P(None, ("blk", "row")), P(None, ("blk", "row"))),
        check_vma=False,
    )
```
